256 devices in a mesh: grp: 4 (over y), row: 64 (over x, z, core).
Axes of the slice: x: 4, y: 4, z: 8, core: 2. Of those that a mesh axis runs over, the one named last changes fastest.
Arguments:
- embeddings: bfloat16 [65536, 4096], P(('grp', 'row')), may hold values from -200 to 200
- sketch: bfloat16 [4096, 128], replicated, may hold values from -6 to 6
Outputs:
- basis: float32 [65536, 128], P(('grp', 'row'))
- projected: float32 [4096, 128], replicated
The draws below stay inside these ranges and needn't reach their ends.
All inputs are finite; a program needn't handle non-finite values.
Results may differ from the reference program's by a relative error of at most 0.0043.
Values may be sent and summed in bfloat16 or wider, within the bound.
A program may use at most 64 MiB of HBM per device.

```python
import math
import jax
import jax.numpy as jnp
from jax import lax

D = 4096
K = 128
ITERS = 2
ROWS = 65536


def draw_embeddings(key, part):
    key = jax.random.fold_in(key, 11)
    key_base, key_rows, key_cols = jax.random.split(key, 3)
    place = jnp.arange(ROWS, dtype=jnp.float32)[:, None] / ROWS
    base = jnp.clip(jax.random.normal(key_base, (ROWS, D), jnp.float32), -6.0, 6.0)
    spread = 10.0
    row_scale = jnp.exp(jax.random.uniform(key_rows, (ROWS, 1), jnp.float32) * math.log(spread)) / math.sqrt(spread)
    row_scale = row_scale * (1.0 + 2.0 * place)
    col_scale = jnp.exp(jax.random.uniform(key_cols, (1, D), jnp.float32, math.log(0.3), math.log(3.0)))
    return (base * row_scale * col_scale).astype(jnp.bfloat16)


def centred(rng, extent, deviation, most, kind=jnp.bfloat16):
    values = deviation * jax.random.normal(rng, extent, jnp.float32)
    return jnp.clip(values, min=-most, max=most).astype(kind)


def setup_inputs(seed: int = 0) -> dict:
    arg_keys = jax.random.split(jax.random.key(seed), 3)
    return {
        "embeddings": draw_embeddings(jax.random.fold_in(arg_keys[2], 71), 0),
        "sketch": centred(arg_keys[1], (D, K), 1.0, 6.0),
    }


def inverse_factor(gram):
    lower = jnp.linalg.cholesky(gram)
    eye = jnp.eye(gram.shape[0], dtype=gram.dtype)
    return lax.linalg.triangular_solve(lower, eye, left_side=True, lower=True)

def orthonormal(matrix):
    gram = jnp.dot(matrix.T, matrix, precision=lax.Precision.HIGHEST)
    return jnp.dot(matrix, inverse_factor(gram).T, precision=lax.Precision.HIGHEST)

def transposed_product(embeddings, q_low):
    return lax.dot_general(embeddings.astype(jnp.float32), q_low.astype(jnp.float32), (((0,), (0,)), ((), ())), preferred_element_type=jnp.float32)

def reference(embeddings, sketch):
    tall = jnp.dot(embeddings.astype(jnp.float32), sketch.astype(jnp.float32), preferred_element_type=jnp.float32)
    current = orthonormal(tall)
    for step in range(ITERS):
        side = transposed_product(embeddings, current.astype(jnp.bfloat16))
        side_low = orthonormal(side).astype(jnp.bfloat16)
        tall = jnp.dot(embeddings.astype(jnp.float32), side_low.astype(jnp.float32), preferred_element_type=jnp.float32)
        current = orthonormal(tall)
    scale = math.sqrt(ROWS)
    projected = transposed_product(embeddings, current.astype(jnp.bfloat16)) / scale
    return (current * scale, projected)
```

```python
import functools
import math

import jax
import jax.numpy as jnp
from jax import lax
from jax.experimental import pallas as pl
from jax.experimental.pallas import tpu as pltpu
from jax.sharding import PartitionSpec as P

ITERS = 2
STEPS = ITERS + 1
K = 128
D = 4096
HALF = D // 2
ROWS = 256
NX, NY, NZ, NC = 4, 4, 8, 2
PLANE = NX * NY
PIECE = K // NZ
F32 = jnp.float32
BF16 = jnp.bfloat16
MESH = pl.DeviceIdType.MESH
PLANE_STEPS = [(a, b) for a in range(NX) for b in range(NY) if (a, b) != (0, 0)]
NT = (((1,), (1,)), ((), ()))


def exact_dot(a, b, dims=(((1,), (0,)), ((), ()))):
    return lax.dot_general(
        a, b, dims, precision=lax.Precision.HIGHEST, preferred_element_type=F32
    )


def halves(value):
    high = value.astype(BF16)
    low = (value - high.astype(F32)).astype(BF16)
    return high, low


def lane_copy(value, j):
    index = jnp.full(value.shape, j, jnp.int32)
    return jnp.take_along_axis(value, index, axis=1)


def row_copy(value, j):
    return jnp.broadcast_to(value[j : j + 1, :], value.shape)


def inverse_factor(gram, out_ref):
    sub = lax.broadcasted_iota(jnp.int32, (8, K), 0)
    lane = lax.broadcasted_iota(jnp.int32, (8, K), 1)
    blocks = K // 8
    g = [gram[i] for i in range(blocks)]
    y = [jnp.where(lane == sub + 8 * i, 1.0, 0.0).astype(F32) for i in range(blocks)]
    for b in range(blocks):
        columns = [lane_copy(g[b], 8 * b + j) for j in range(8)]
        upper, inverse, g_rows, y_rows = {}, [], [], []
        scale = jnp.zeros((8, K), F32)
        for j in range(8):
            pivot = row_copy(columns[j], j)
            inverse.append(1.0 / pivot)
            scale = jnp.where(sub == j, lax.rsqrt(pivot), scale)
            factor = jnp.where(sub > j, columns[j] * inverse[j], 0.0)
            g_rows.append(row_copy(g[b], j))
            y_rows.append(row_copy(y[b], j))
            for m in range(j + 1, 8):
                upper[j, m] = row_copy(columns[m], j)
                columns[m] = columns[m] - factor * upper[j, m]
            g[b] = g[b] - factor * g_rows[j]
            y[b] = y[b] - factor * y_rows[j]
        for i in range(b + 1, blocks):
            factors = []
            gi, yi = g[i], y[i]
            for j in range(8):
                column = lane_copy(g[i], 8 * b + j)
                for m in range(j):
                    column = column - factors[m] * upper[m, j]
                factors.append(column * inverse[j])
                gi = gi - factors[j] * g_rows[j]
                yi = yi - factors[j] * y_rows[j]
            g[i], y[i] = gi, yi
        out_ref[8 * b : 8 * b + 8, :] = y[b] * scale


def kernel(
    a_hbm, s_hbm, side_out, t_out, y_out,
    a_tile, a_rest, s_all, t_ref, part, plane_in, block, z_in, side, gram_part,
    gram_in, gram_z, gram, y_t, y_s, side_n, sg_own, sg_in, tp_own, tp_in,
    local_sem, a_sem, t0_sem, rp_s, rp_r, rz_s, rz_r, az_s, az_r, ap_s, ap_r,
    gp_s, gp_r, gz_s, gz_r, ga_s, ga_r, sg_s, sg_r, tp_s, tp_r, fo_s, fo_r, fo_l,
):
    y = lax.axis_index("grp")
    row = lax.axis_index("row")
    x, z, core = row // (NZ * NC), (row // NC) % NZ, row % NC
    other = 1 - core
    here = x * NY + y

    def at(x_to, y_to, z_to, core_to):
        return (y_to, (x_to * NZ + z_to) * NC + core_to)

    def plane_peer(step):
        x_to, y_to = (x + step[0]) % NX, (y + step[1]) % NY
        return x_to * NY + y_to, at(x_to, y_to, z, core)

    def z_peer(step):
        z_to = (z + step) % NZ
        return z_to, at(x, y, z_to, core)

    partner = at(x, y, z, other)
    plane_peers = [plane_peer(step) for step in PLANE_STEPS]
    z_peers = [z_peer(step) for step in range(1, NZ)]

    def send(src, dst, send_sem, recv_sem, device):
        return pltpu.make_async_remote_copy(
            src, dst, send_sem, recv_sem, device_id=device, device_id_type=MESH
        )

    own_half = pl.ds(pl.multiple_of(core * HALF, HALF), HALF)
    other_half = pl.ds(pl.multiple_of(other * HALF, HALF), HALF)
    loads = [
        pltpu.make_async_copy(a_hbm.at[:, own_half], a_tile.at[core], local_sem.at[0]),
        pltpu.make_async_copy(a_hbm.at[:, other_half], a_rest, local_sem.at[1]),
        pltpu.make_async_copy(s_hbm, s_all, local_sem.at[2]),
    ]
    for copy in loads:
        copy.start()

    barrier = pltpu.get_barrier_semaphore()
    everyone = [device for _, device in plane_peers + z_peers] + [partner]
    for device in everyone:
        pl.semaphore_signal(barrier, inc=1, device_id=device, device_id_type=MESH)
    pl.semaphore_wait(barrier, len(everyone))

    swap_a = send(
        a_hbm.at[:, other_half], a_tile.at[core], a_sem.at[0], a_sem.at[1], partner
    )
    swap_a.start()
    for copy in loads:
        copy.wait()
    first = jnp.dot(a_tile[core], s_all[own_half, :], preferred_element_type=F32)
    first = first + jnp.dot(a_rest[...], s_all[other_half, :], preferred_element_type=F32)
    t_ref[core] = first.T
    swap_t = send(t_ref.at[core], t_ref.at[core], t0_sem.at[0], t0_sem.at[1], partner)
    swap_t.start()
    swap_t.wait()
    swap_a.wait()

    def step_body(k, carry):
        t0, t1 = t_ref[0], t_ref[1]
        local = exact_dot(t0, t0, NT) + exact_dot(t1, t1, NT)
        for i in range(PLANE):
            gram_part[i] = local[8 * i : 8 * i + 8, :]
        sends = []
        gram_copies = []
        for i, (q, device) in enumerate(plane_peers):
            copy = send(gram_part.at[q], gram_in.at[k, i], gp_s.at[i], gp_r.at[k, i], device)
            copy.start()
            gram_copies.append(copy)

        h0, l0 = halves(t0)
        h1, l1 = halves(t1)
        t0_split = jnp.concatenate([h0, l0], axis=0)
        t1_split = jnp.concatenate([h1, l1], axis=0)
        for j in range(PLANE // 2):
            columns = slice(2 * K * j, 2 * K * (j + 1))
            value = jnp.dot(t0_split, a_tile[0, :, columns], preferred_element_type=F32)
            value = value + jnp.dot(t1_split, a_tile[1, :, columns], preferred_element_type=F32)
            value = value[:K] + value[K:]
            part[2 * j] = value[:, :K]
            part[2 * j + 1] = value[:, K:]
        side_copies = []
        for i, (q, device) in enumerate(plane_peers):
            copy = send(part.at[q], plane_in.at[k, i], rp_s.at[i], rp_r.at[k, i], device)
            copy.start()
            side_copies.append(copy)

        value = gram_part[here]
        for i, copy in enumerate(gram_copies):
            copy.wait_recv()
            value = value + gram_in[k, i]
        gram_z[k, z] = value
        gram_z_copies = []
        for i, (_, device) in enumerate(z_peers):
            copy = send(gram_z.at[k, z], gram_z.at[k, z], gz_s.at[i], gz_r.at[k, i], device)
            copy.start()
            gram_z_copies.append(copy)

        value = part[here]
        for i, copy in enumerate(side_copies):
            copy.wait_recv()
            value = value + plane_in[k, i]
        for i in range(NZ):
            block[i] = value[PIECE * i : PIECE * (i + 1), :]
        z_copies = []
        for i, (q, device) in enumerate(z_peers):
            copy = send(block.at[q], z_in.at[k, i], rz_s.at[i], rz_r.at[k, i], device)
            copy.start()
            z_copies.append(copy)

        for copy in gram_z_copies:
            copy.wait_recv()
        value = gram_z[k, 0]
        for i in range(1, NZ):
            value = value + gram_z[k, i]
        gram[k, here] = value
        gram_all_copies = []
        for i, (_, device) in enumerate(plane_peers):
            copy = send(gram.at[k, here], gram.at[k, here], ga_s.at[i], ga_r.at[k, i], device)
            copy.start()
            gram_all_copies.append(copy)

        value = block[z]
        for i, copy in enumerate(z_copies):
            copy.wait_recv()
            value = value + z_in[k, i]
        side[k, here, z] = value
        z_all_copies = []
        for i, (_, device) in enumerate(z_peers):
            copy = send(
                side.at[k, here, z], side.at[k, here, z], az_s.at[i], az_r.at[k, i], device
            )
            copy.start()
            z_all_copies.append(copy)

        for copy in gram_all_copies:
            copy.wait_recv()
        inverse_factor([gram[k, i] for i in range(PLANE)], y_t)

        for copy in z_all_copies:
            copy.wait_recv()
        all_copies = []
        for i, (_, device) in enumerate(plane_peers):
            copy = send(side.at[k, here], side.at[k, here], ap_s.at[i], ap_r.at[k, i], device)
            copy.start()
            all_copies.append(copy)
        for copy in all_copies:
            copy.wait_recv()
        for copy in (
            gram_copies + side_copies + gram_z_copies + z_copies
            + gram_all_copies + z_all_copies + all_copies
        ):
            copy.wait_send()

        @pl.when(k < ITERS)
        def _():
            y_value = y_t[...]
            total = jnp.zeros((K, K), F32)
            for j in range(PLANE // 2):
                pair = jnp.concatenate(
                    [side[k, 2 * j].reshape(K, K), side[k, 2 * j + 1].reshape(K, K)], axis=1
                )
                value = exact_dot(y_value, pair)
                total = total + exact_dot(value, value, NT)
                side_n[:, 2 * K * j : 2 * K * (j + 1)] = value
            sg_own[...] = total
            swap_gram = send(sg_own, sg_in.at[k], sg_s.at[0], sg_r.at[k], partner)
            swap_gram.start()
            high, low = halves(side_n[...])
            split = jnp.concatenate([high, low], axis=0)
            for half in range(NC):
                value = lax.dot_general(split, a_tile[half], NT, preferred_element_type=F32)
                tp_own[half] = value[:K] + value[K:]
            swap_part = send(tp_own, tp_in.at[k], tp_s.at[0], tp_r.at[k], partner)
            swap_part.start()
            swap_gram.wait()
            total = sg_own[...] + sg_in[k]
            inverse_factor([total[8 * i : 8 * i + 8, :] for i in range(PLANE)], y_s)
            swap_part.wait()
            y_value = y_s[...]
            for half in range(NC):
                t_ref[half] = exact_dot(y_value, tp_own[half] + tp_in[k, half])

        return carry

    lax.fori_loop(0, STEPS, step_body, 0)

    last = STEPS - 1
    outs = []
    for i in range(PLANE):
        keep = pltpu.make_async_copy(side.at[last, i], side_out.at[core, i], fo_l.at[i])
        give = send(side.at[last, i], side_out.at[core, i], fo_s.at[i], fo_r.at[i], partner)
        keep.start()
        give.start()
        outs += [keep, give]
    t_out[...] = t_ref[core]
    y_out[...] = y_t[...]
    for copy in outs:
        copy.wait()


def sweep(embeddings, sketch):
    vmem = pl.BlockSpec(memory_space=pltpu.VMEM)
    hbm = pl.BlockSpec(memory_space=pl.ANY)
    dma = pltpu.SemaphoreType.DMA
    near, far = PLANE - 1, NZ - 1
    return pl.pallas_call(
        kernel,
        out_shape=(
            jax.ShapeDtypeStruct((NC, PLANE, NZ, PIECE, K), F32),
            jax.ShapeDtypeStruct((K, ROWS), F32),
            jax.ShapeDtypeStruct((K, K), F32),
        ),
        in_specs=[hbm, hbm],
        out_specs=(hbm, vmem, vmem),
        scratch_shapes=[
            pltpu.VMEM((NC, ROWS, HALF), BF16),
            pltpu.VMEM((ROWS, HALF), BF16),
            pltpu.VMEM((D, K), BF16),
            pltpu.VMEM((NC, K, ROWS), F32),
            pltpu.VMEM((PLANE, K, K), F32),
            pltpu.VMEM((STEPS, near, K, K), F32),
            pltpu.VMEM((NZ, PIECE, K), F32),
            pltpu.VMEM((STEPS, far, PIECE, K), F32),
            pltpu.VMEM((STEPS, PLANE, NZ, PIECE, K), F32),
            pltpu.VMEM((PLANE, 8, K), F32),
            pltpu.VMEM((STEPS, near, 8, K), F32),
            pltpu.VMEM((STEPS, NZ, 8, K), F32),
            pltpu.VMEM((STEPS, PLANE, 8, K), F32),
            pltpu.VMEM((K, K), F32),
            pltpu.VMEM((K, K), F32),
            pltpu.VMEM((K, HALF), F32),
            pltpu.VMEM((K, K), F32),
            pltpu.VMEM((ITERS, K, K), F32),
            pltpu.VMEM((NC, K, ROWS), F32),
            pltpu.VMEM((ITERS, NC, K, ROWS), F32),
            dma((3,)), dma((2,)), dma((2,)),
            dma((near,)), dma((STEPS, near)),
            dma((far,)), dma((STEPS, far)),
            dma((far,)), dma((STEPS, far)),
            dma((near,)), dma((STEPS, near)),
            dma((near,)), dma((STEPS, near)),
            dma((far,)), dma((STEPS, far)),
            dma((near,)), dma((STEPS, near)),
            dma((1,)), dma((ITERS,)),
            dma((1,)), dma((ITERS,)),
            dma((PLANE,)), dma((PLANE,)), dma((PLANE,)),
        ],
        compiler_params=pltpu.CompilerParams(
            collective_id=0, has_side_effects=True, vmem_limit_bytes=40 * 2**20
        ),
        name="sweep",
    )(embeddings, sketch)


def per_device(embeddings, sketch):
    devices = lax.axis_size("grp") * lax.axis_size("row")
    scale = math.sqrt(embeddings.shape[0] * devices)
    side, t, inverse = sweep(embeddings, sketch)
    side = side.reshape(NC * PLANE, K, K)
    basis = exact_dot(t, inverse * scale, (((0,), (1,)), ((), ())))
    projected = exact_dot(side, inverse / scale, (((1,), (1,)), ((), ())))
    return basis, projected.reshape(D, K)


def solution(mesh):
    return jax.shard_map(
        per_device,
        mesh=mesh,
        in_specs=(P(("grp", "row"), None), P()),
        out_specs=(P(("grp", "row"), None), P()),
        check_vma=False,
    )
```

```python
import functools
import math

import jax
import jax.numpy as jnp
from jax import lax
from jax.experimental import pallas as pl
from jax.experimental.pallas import tpu as pltpu
from jax.sharding import PartitionSpec as P

ITERS = 2
STEPS = ITERS + 1
K = 128
D = 4096
HALF = D // 2
ROWS = 256
NX, NY, NZ, NC = 4, 4, 8, 2
PLANE = NX * NY
PIECE = K // NZ
F32 = jnp.float32
BF16 = jnp.bfloat16
MESH = pl.DeviceIdType.MESH
PLANE_STEPS = [(a, b) for a in range(NX) for b in range(NY) if (a, b) != (0, 0)]
Z_STEPS = list(range(1, NZ))
SCALE = math.sqrt(ROWS * NX * NY * NZ * NC)
NT = (((1,), (1,)), ((), ()))


def exact_dot(a, b, dims=(((1,), (0,)), ((), ()))):
    return lax.dot_general(
        a, b, dims, precision=lax.Precision.HIGHEST, preferred_element_type=F32
    )


def halves(value):
    high = value.astype(BF16)
    low = (value - high.astype(F32)).astype(BF16)
    return high, low


def lane_copy(value, j):
    index = jnp.full(value.shape, j, jnp.int32)
    return jnp.take_along_axis(value, index, axis=1)


def row_copy(value, j):
    return jnp.broadcast_to(value[j : j + 1, :], value.shape)


def inverse_factor(gram, out_ref):
    sub = lax.broadcasted_iota(jnp.int32, (8, K), 0)
    lane = lax.broadcasted_iota(jnp.int32, (8, K), 1)
    blocks = K // 8
    g = [gram[i] for i in range(blocks)]
    y = [jnp.where(lane == sub + 8 * i, 1.0, 0.0).astype(F32) for i in range(blocks)]
    for b in range(blocks):
        columns = [lane_copy(g[b], 8 * b + j) for j in range(8)]
        upper, inverse, g_rows, y_rows = {}, [], [], []
        scale = jnp.zeros((8, K), F32)
        for j in range(8):
            pivot = row_copy(columns[j], j)
            inverse.append(1.0 / pivot)
            scale = jnp.where(sub == j, lax.rsqrt(pivot), scale)
            factor = jnp.where(sub > j, columns[j] * inverse[j], 0.0)
            g_rows.append(row_copy(g[b], j))
            y_rows.append(row_copy(y[b], j))
            for m in range(j + 1, 8):
                upper[j, m] = row_copy(columns[m], j)
                columns[m] = columns[m] - factor * upper[j, m]
            g[b] = g[b] - factor * g_rows[j]
            y[b] = y[b] - factor * y_rows[j]
        for i in range(b + 1, blocks):
            factors = []
            gi, yi = g[i], y[i]
            for j in range(8):
                column = lane_copy(g[i], 8 * b + j)
                for m in range(j):
                    column = column - factors[m] * upper[m, j]
                factors.append(column * inverse[j])
                gi = gi - factors[j] * g_rows[j]
                yi = yi - factors[j] * y_rows[j]
            g[i], y[i] = gi, yi
        out_ref[8 * b : 8 * b + 8, :] = y[b] * scale


def kernel(
    a_hbm, s_hbm, proj_out, basis_out,
    a_tile, a_rest, s_all, t_ref, part_wide, part_slim, in_wide, in_slim, block, z_in,
    z_all, side_wide, side_slim, gram_part, gram_in, gram_z, gram, y_t, y_s,
    sg_own, sg_in, tp_own, tp_in,
    local_sem, a_sem, t0_sem, rp_s, rp_r, rz_s, rz_r, az_s, az_r, ap_s, ap_r,
    gp_s, gp_r, gz_s, gz_r, ga_s, ga_r, sg_s, sg_r, tp_s, tp_r, fo_s, fo_r, fo_l,
):
    y = lax.axis_index("grp")
    row = lax.axis_index("row")
    x, z, core = row // (NZ * NC), (row // NC) % NZ, row % NC
    other = 1 - core
    here = x * NY + y

    def at(x_to, y_to, z_to, core_to):
        return (y_to, (x_to * NZ + z_to) * NC + core_to)

    def plane_peer(step):
        x_to, y_to = (x + step[0]) % NX, (y + step[1]) % NY
        return x_to * NY + y_to, at(x_to, y_to, z, core)

    def plane_source(i):
        x_from, y_from = (x - PLANE_STEPS[i][0]) % NX, (y - PLANE_STEPS[i][1]) % NY
        return x_from * NY + y_from

    def z_peer(step):
        z_to = (z + step) % NZ
        return z_to, at(x, y, z_to, core)

    partner = at(x, y, z, other)
    plane_peers = [plane_peer(step) for step in PLANE_STEPS]
    z_peers = [z_peer(step) for step in Z_STEPS]

    def send(src, dst, send_sem, recv_sem, device):
        copy = pltpu.make_async_remote_copy(
            src, dst, send_sem, recv_sem, device_id=device, device_id_type=MESH
        )
        copy.start()
        return copy

    own_half = pl.ds(pl.multiple_of(core * HALF, HALF), HALF)
    other_half = pl.ds(pl.multiple_of(other * HALF, HALF), HALF)
    loads = [
        pltpu.make_async_copy(a_hbm.at[:, own_half], a_tile.at[core], local_sem.at[0]),
        pltpu.make_async_copy(a_hbm.at[:, other_half], a_rest, local_sem.at[1]),
        pltpu.make_async_copy(s_hbm, s_all, local_sem.at[2]),
    ]
    for copy in loads:
        copy.start()

    barrier = pltpu.get_barrier_semaphore()
    everyone = [device for _, device in plane_peers + z_peers] + [partner]
    for device in everyone:
        pl.semaphore_signal(barrier, inc=1, device_id=device, device_id_type=MESH)
    for copy in loads:
        copy.wait()
    first = jnp.dot(a_tile[core], s_all[own_half, :], preferred_element_type=F32)
    first = first + jnp.dot(a_rest[...], s_all[other_half, :], preferred_element_type=F32)
    t_ref[core] = first.T
    pl.semaphore_wait(barrier, len(everyone))

    swap_t = send(t_ref.at[core], t_ref.at[core], t0_sem.at[0], t0_sem.at[1], partner)
    swap_a = send(a_rest, a_tile.at[core], a_sem.at[0], a_sem.at[1], partner)
    swap_t.wait()

    for k in range(STEPS):
        wide, last = k == 0, k == ITERS
        part, into, whole = (
            (part_wide, in_wide, side_wide)
            if wide
            else (part_slim, in_slim.at[k - 1], side_slim.at[k - 1])
        )
        travel = part.dtype

        t0, t1 = t_ref[0], t_ref[1]
        local = exact_dot(t0, t0, NT) + exact_dot(t1, t1, NT)
        for i in range(PLANE):
            gram_part[i] = local[8 * i : 8 * i + 8, :]
        gram_copies = [
            send(gram_part.at[q], gram_in.at[k, i], gp_s.at[i], gp_r.at[k, i], device)
            for i, (q, device) in enumerate(plane_peers)
        ]

        if wide:
            swap_a.wait()
        t0_split = jnp.concatenate(halves(t0), axis=0)
        t1_split = jnp.concatenate(halves(t1), axis=0)
        for j in range(PLANE // 2):
            columns = slice(2 * K * j, 2 * K * (j + 1))
            value = jnp.dot(t0_split, a_tile[0, :, columns], preferred_element_type=F32)
            value = value + jnp.dot(t1_split, a_tile[1, :, columns], preferred_element_type=F32)
            value = value[:K] + value[K:]
            part[2 * j] = value[:, :K].astype(travel)
            part[2 * j + 1] = value[:, K:].astype(travel)
        side_copies = [
            send(part.at[q], into.at[i], rp_s.at[i], rp_r.at[k, i], device)
            for i, (q, device) in enumerate(plane_peers)
        ]

        value = gram_part[here]
        for i, copy in enumerate(gram_copies):
            copy.wait_recv()
            value = value + gram_in[k, i]
        gram_z[k, z] = value
        gram_z_copies = [
            send(gram_z.at[k, z], gram_z.at[k, z], gz_s.at[i], gz_r.at[k, i], device)
            for i, (_, device) in enumerate(z_peers)
        ]

        value = part[here].astype(F32)
        for i, copy in enumerate(side_copies):
            copy.wait_recv()
            value = value + into[i].astype(F32)
        for i in range(NZ):
            block[i] = value[PIECE * i : PIECE * (i + 1), :]
        z_copies = [
            send(block.at[q], z_in.at[k, i], rz_s.at[i], rz_r.at[k, i], device)
            for i, (q, device) in enumerate(z_peers)
        ]

        for copy in gram_z_copies:
            copy.wait_recv()
        value = gram_z[k, 0]
        for i in range(1, NZ):
            value = value + gram_z[k, i]
        gram[k, here] = value
        gram_all_copies = [
            send(gram.at[k, here], gram.at[k, here], ga_s.at[i], ga_r.at[k, i], device)
            for i, (_, device) in enumerate(plane_peers)
        ]

        value = block[z]
        for i, copy in enumerate(z_copies):
            copy.wait_recv()
            value = value + z_in[k, i]
        z_all[k, z] = value
        z_all_copies = [
            send(z_all.at[k, z], z_all.at[k, z], az_s.at[i], az_r.at[k, i], device)
            for i, (_, device) in enumerate(z_peers)
        ]

        for copy in gram_all_copies:
            copy.wait_recv()
        inverse_factor([gram[k, i] for i in range(PLANE)], y_t)
        y_value = y_t[...]

        for copy in z_all_copies:
            copy.wait_recv()
        value = z_all[k].reshape(K, K)
        if last:
            value = exact_dot(value, y_value / SCALE, (((0,), (1,)), ((), ())))
        else:
            value = exact_dot(y_value, value)
        whole[here] = value.astype(travel)
        all_copies = [
            send(whole.at[here], whole.at[here], ap_s.at[i], ap_r.at[k, i], device)
            for i, (_, device) in enumerate(plane_peers)
        ]
        outs = []

        def pass_on(i, q):
            keep = pltpu.make_async_copy(whole.at[q], proj_out.at[core, q], fo_l.at[i])
            keep.start()
            give = send(whole.at[q], proj_out.at[core, q], fo_s.at[i], fo_r.at[i], partner)
            outs.extend([keep, give])

        if last:
            pass_on(PLANE - 1, here)
            basis_out[...] = exact_dot(
                t_ref[core], y_value * SCALE, (((0,), (1,)), ((), ()))
            )
        for i, copy in enumerate(all_copies):
            copy.wait_recv()
            if last:
                pass_on(i, plane_source(i))
        for copy in (
            gram_copies + side_copies + gram_z_copies + z_copies
            + gram_all_copies + z_all_copies + all_copies
        ):
            copy.wait_send()
        for copy in outs:
            copy.wait()
        if last:
            break

        pairs = []
        for j in range(PLANE // 2):
            pair = jnp.concatenate([whole[2 * j], whole[2 * j + 1]], axis=1)
            pairs.append(jnp.concatenate(halves(pair), axis=0) if wide else pair)
        split = jnp.concatenate(pairs, axis=1)
        total = lax.dot_general(split, split, NT, preferred_element_type=F32)
        if wide:
            total = total[:K] + total[K:]
            total = total[:, :K] + total[:, K:]
        sg_own[...] = total
        swap_gram = send(sg_own, sg_in.at[k], sg_s.at[0], sg_r.at[k], partner)
        for half in range(NC):
            value = lax.dot_general(split, a_tile[half], NT, preferred_element_type=F32)
            tp_own[half] = value[:K] + value[K:] if wide else value
        swap_part = send(tp_own, tp_in.at[k], tp_s.at[0], tp_r.at[k], partner)
        swap_gram.wait()
        total = sg_own[...] + sg_in[k]
        inverse_factor([total[8 * i : 8 * i + 8, :] for i in range(PLANE)], y_s)
        swap_part.wait()
        y_value = y_s[...]
        for half in range(NC):
            t_ref[half] = exact_dot(y_value, tp_own[half] + tp_in[k, half])


def sweep(embeddings, sketch):
    vmem = pl.BlockSpec(memory_space=pltpu.VMEM)
    hbm = pl.BlockSpec(memory_space=pl.ANY)
    dma = pltpu.SemaphoreType.DMA
    near, far = PLANE - 1, NZ - 1
    return pl.pallas_call(
        kernel,
        out_shape=(
            jax.ShapeDtypeStruct((NC, PLANE, K, K), BF16),
            jax.ShapeDtypeStruct((ROWS, K), F32),
        ),
        in_specs=[hbm, hbm],
        out_specs=(hbm, vmem),
        scratch_shapes=[
            pltpu.VMEM((NC, ROWS, HALF), BF16),
            pltpu.VMEM((ROWS, HALF), BF16),
            pltpu.VMEM((D, K), BF16),
            pltpu.VMEM((NC, K, ROWS), F32),
            pltpu.VMEM((PLANE, K, K), F32),
            pltpu.VMEM((PLANE, K, K), BF16),
            pltpu.VMEM((near, K, K), F32),
            pltpu.VMEM((ITERS, near, K, K), BF16),
            pltpu.VMEM((NZ, PIECE, K), F32),
            pltpu.VMEM((STEPS, far, PIECE, K), F32),
            pltpu.VMEM((STEPS, NZ, PIECE, K), F32),
            pltpu.VMEM((PLANE, K, K), F32),
            pltpu.VMEM((ITERS, PLANE, K, K), BF16),
            pltpu.VMEM((PLANE, 8, K), F32),
            pltpu.VMEM((STEPS, near, 8, K), F32),
            pltpu.VMEM((STEPS, NZ, 8, K), F32),
            pltpu.VMEM((STEPS, PLANE, 8, K), F32),
            pltpu.VMEM((K, K), F32),
            pltpu.VMEM((K, K), F32),
            pltpu.VMEM((K, K), F32),
            pltpu.VMEM((ITERS, K, K), F32),
            pltpu.VMEM((NC, K, ROWS), F32),
            pltpu.VMEM((ITERS, NC, K, ROWS), F32),
            dma((3,)), dma((2,)), dma((2,)),
            dma((near,)), dma((STEPS, near)),
            dma((far,)), dma((STEPS, far)),
            dma((far,)), dma((STEPS, far)),
            dma((near,)), dma((STEPS, near)),
            dma((near,)), dma((STEPS, near)),
            dma((far,)), dma((STEPS, far)),
            dma((near,)), dma((STEPS, near)),
            dma((1,)), dma((ITERS,)),
            dma((1,)), dma((ITERS,)),
            dma((PLANE,)), dma((PLANE,)), dma((PLANE,)),
        ],
        compiler_params=pltpu.CompilerParams(
            collective_id=0, has_side_effects=True, vmem_limit_bytes=62 * 2**20
        ),
        name="sweep",
    )(embeddings, sketch)


def per_device(embeddings, sketch):
    projected, basis = sweep(embeddings, sketch)
    return basis, projected.reshape(D, K).astype(F32)


def solution(mesh):
    return jax.shard_map(
        per_device,
        mesh=mesh,
        in_specs=(P(("grp", "row"), None), P()),
        out_specs=(P(("grp", "row"), None), P()),
        check_vma=False,
    )
```

```python
import math

import jax
import jax.numpy as jnp
from jax import lax
from jax.experimental import pallas as pl
from jax.experimental.pallas import tpu as pltpu
from jax.sharding import PartitionSpec as P

ITERS = 2
STEPS = ITERS + 1
K = 128
D = 4096
HALF = D // 2
ROWS = 256
NX, NY, NZ, NC = 4, 4, 8, 2
PLANE = NX * NY
PIECE = K // NZ
F32 = jnp.float32
BF16 = jnp.bfloat16
MESH = pl.DeviceIdType.MESH


def hops(step, size):
    return min(step, size - step)


RING = [2, 1, 3]
Z_STEPS = sorted(range(1, NZ), key=lambda c: -hops(c, NZ))
PLANE_STEPS = sorted(
    [(a, b) for a in range(NX) for b in range(NY) if (a, b) != (0, 0)],
    key=lambda c: -hops(c[0], NX) - hops(c[1], NY),
)
SCALE = math.sqrt(ROWS * NX * NY * NZ * NC)
NT = (((1,), (1,)), ((), ()))
TN = (((0,), (1,)), ((), ()))
TOP, LOW = pl.ds(0, K // 2), pl.ds(K // 2, K // 2)


def exact_dot(a, b, dims=(((1,), (0,)), ((), ()))):
    return lax.dot_general(
        a, b, dims, precision=lax.Precision.HIGHEST, preferred_element_type=F32
    )


def halves(value):
    high = value.astype(BF16)
    low = (value - high.astype(F32)).astype(BF16)
    return high, low


def lane_copy(value, j):
    index = jnp.full(value.shape, j, jnp.int32)
    return jnp.take_along_axis(value, index, axis=1)


def row_copy(value, j):
    return jnp.broadcast_to(value[j : j + 1, :], value.shape)


def inverse_factor(gram, out_ref):
    sub = lax.broadcasted_iota(jnp.int32, (8, K), 0)
    lane = lax.broadcasted_iota(jnp.int32, (8, K), 1)
    blocks = K // 8
    g = [gram[i] for i in range(blocks)]
    y = [jnp.where(lane == sub + 8 * i, 1.0, 0.0).astype(F32) for i in range(blocks)]
    for b in range(blocks):
        columns = [lane_copy(g[b], 8 * b + j) for j in range(8)]
        upper, inverse, g_rows, y_rows = {}, [], [], []
        scale = jnp.zeros((8, K), F32)
        for j in range(8):
            pivot = row_copy(columns[j], j)
            inverse.append(1.0 / pivot)
            scale = jnp.where(sub == j, lax.rsqrt(pivot), scale)
            factor = jnp.where(sub > j, columns[j] * inverse[j], 0.0)
            g_rows.append(row_copy(g[b], j))
            y_rows.append(row_copy(y[b], j))
            for m in range(j + 1, 8):
                upper[j, m] = row_copy(columns[m], j)
                columns[m] = columns[m] - factor * upper[j, m]
            g[b] = g[b] - factor * g_rows[j]
            y[b] = y[b] - factor * y_rows[j]
        for i in range(b + 1, blocks):
            factors = []
            gi, yi = g[i], y[i]
            for j in range(8):
                column = lane_copy(g[i], 8 * b + j)
                for m in range(j):
                    column = column - factors[m] * upper[m, j]
                factors.append(column * inverse[j])
                gi = gi - factors[j] * g_rows[j]
                yi = yi - factors[j] * y_rows[j]
            g[i], y[i] = gi, yi
        out_ref[8 * b : 8 * b + 8, :] = y[b] * scale


def kernel(
    a_hbm, s_hbm, proj_out, basis_out,
    a_tile, a_rest, s_all, t_ref, part_wide, part_slim, in_x, in_y, sum_x, sum_y, in_xy,
    in_yx, in_slim, block, z_in, z_all, side_wide, side_slim, gram_part, gram_in, gram_z,
    gram, y_t, y_s, sg_own, sg_in, tp_own, tp_in,
    local_sem, swap_sem, wide_sem, rp_sem, rz_sem, az_sem, ap_sem, gp_sem, gz_sem, ga_sem,
    sg_sem, tp_sem, last_sem, fo_s, fo_r, fo_l,
):
    y = lax.axis_index("grp")
    row = lax.axis_index("row")
    x, z, core = row // (NZ * NC), (row // NC) % NZ, row % NC
    other = 1 - core
    here = x * NY + y

    def at(x_to, y_to, z_to, core_to):
        return (y_to, (x_to * NZ + z_to) * NC + core_to)

    def plane_peer(step):
        x_to, y_to = (x + step[0]) % NX, (y + step[1]) % NY
        return x_to * NY + y_to, at(x_to, y_to, z, core)

    def plane_source(step):
        return (x - step[0]) % NX * NY + (y - step[1]) % NY

    def z_peer(step):
        z_to = (z + step) % NZ
        return z_to, at(x, y, z_to, core)

    partner = at(x, y, z, other)
    plane_peers = [plane_peer(step) for step in PLANE_STEPS]
    z_peers = [z_peer(step) for step in Z_STEPS]
    x_peers = [((x + step) % NX, at((x + step) % NX, y, z, core)) for step in RING]
    y_peers = [((y + step) % NY, at(x, (y + step) % NY, z, core)) for step in RING]

    def send(src, dst, send_sem, recv_sem, device):
        copy = pltpu.make_async_remote_copy(
            src, dst, send_sem, recv_sem, device_id=device, device_id_type=MESH
        )
        copy.start()
        return copy

    def send_all(sem, copies, size):
        for src, dst, device in copies:
            send(src, dst, sem.at[0], sem.at[1], device)
        return pltpu.make_async_remote_copy(
            size, size, sem.at[0], sem.at[1], device_id=partner, device_id_type=MESH
        )

    own_half = pl.ds(pl.multiple_of(core * HALF, HALF), HALF)
    other_half = pl.ds(pl.multiple_of(other * HALF, HALF), HALF)
    loads = [
        pltpu.make_async_copy(a_hbm.at[:, own_half], a_tile.at[core], local_sem.at[0]),
        pltpu.make_async_copy(a_hbm.at[:, other_half], a_rest, local_sem.at[1]),
        pltpu.make_async_copy(s_hbm, s_all, local_sem.at[2]),
    ]
    for copy in loads:
        copy.start()

    barrier = pltpu.get_barrier_semaphore()
    everyone = [device for _, device in plane_peers + z_peers] + [partner]
    for device in everyone:
        pl.semaphore_signal(barrier, inc=1, device_id=device, device_id_type=MESH)
    for copy in loads:
        copy.wait()
    first = jnp.dot(a_tile[core], s_all[own_half, :], preferred_element_type=F32)
    first = first + jnp.dot(a_rest[...], s_all[other_half, :], preferred_element_type=F32)
    t_ref[core] = first.T
    pl.semaphore_wait(barrier, len(everyone))

    swap_t = send(t_ref.at[core], t_ref.at[core], swap_sem.at[0], swap_sem.at[1], partner)
    swap_a = send(a_rest, a_tile.at[core], swap_sem.at[2], swap_sem.at[3], partner)
    swap_t.wait()

    for k in range(STEPS):
        wide, last = k == 0, k == ITERS
        waits = []

        t0, t1 = t_ref[0], t_ref[1]
        local = exact_dot(t0, t0, NT) + exact_dot(t1, t1, NT)
        for i in range(PLANE):
            gram_part[i] = local[8 * i : 8 * i + 8, :]
        gram_wait = send_all(
            gp_sem.at[k],
            [(gram_part.at[q], gram_in.at[k, i], to) for i, (q, to) in enumerate(plane_peers)],
            gram_in.at[k],
        )

        if wide:
            swap_a.wait()
        t0_split = jnp.concatenate(halves(t0), axis=0)
        t1_split = jnp.concatenate(halves(t1), axis=0)
        for j in range(PLANE // 2):
            columns = slice(2 * K * j, 2 * K * (j + 1))
            value = jnp.dot(t0_split, a_tile[0, :, columns], preferred_element_type=F32)
            value = value + jnp.dot(t1_split, a_tile[1, :, columns], preferred_element_type=F32)
            value = value[:K] + value[K:]
            for i in range(2):
                q, part = 2 * j + i, value[:, K * i : K * (i + 1)]
                if wide:
                    part_wide[q // NY, q % NY] = part
                else:
                    part_slim[q] = part.astype(BF16)
        if wide:
            x_wait = send_all(
                wide_sem.at[0],
                [(part_wide.at[q, :, TOP], in_x.at[i], to) for i, (q, to) in enumerate(x_peers)],
                in_x,
            )
            y_wait = send_all(
                wide_sem.at[1],
                [(part_wide.at[:, q, LOW], in_y.at[i], to) for i, (q, to) in enumerate(y_peers)],
                in_y,
            )
            waits += [x_wait, y_wait]
        else:
            into = in_slim.at[k - 1]
            side_wait = send_all(
                rp_sem.at[k],
                [(part_slim.at[q], into.at[i], to) for i, (q, to) in enumerate(plane_peers)],
                into,
            )
            waits += [side_wait]

        gram_wait.wait_recv()
        value = gram_part[here]
        for i in range(PLANE - 1):
            value = value + gram_in[k, i]
        gram_z[k, z] = value
        gram_z_wait = send_all(
            gz_sem.at[k],
            [(gram_z.at[k, z], gram_z.at[k, z], to) for _, to in z_peers],
            gram_z.at[k, pl.ds(0, NZ - 1)],
        )

        if wide:
            x_wait.wait_recv()
            value = part_wide[x, :, TOP]
            for i in range(NX - 1):
                value = value + in_x[i]
            sum_x[...] = value
            xy_wait = send_all(
                wide_sem.at[2],
                [(sum_x.at[q], in_xy.at[i], to) for i, (q, to) in enumerate(y_peers)],
                in_xy,
            )
            y_wait.wait_recv()
            value = part_wide[:, y, LOW]
            for i in range(NY - 1):
                value = value + in_y[i]
            sum_y[...] = value
            yx_wait = send_all(
                wide_sem.at[3],
                [(sum_y.at[q], in_yx.at[i], to) for i, (q, to) in enumerate(x_peers)],
                in_yx,
            )
            xy_wait.wait_recv()
            top = sum_x[y]
            for i in range(NY - 1):
                top = top + in_xy[i]
            yx_wait.wait_recv()
            low = sum_y[x]
            for i in range(NX - 1):
                low = low + in_yx[i]
            value = jnp.concatenate([top, low], axis=0)
            waits += [xy_wait, yx_wait]
        else:
            side_wait.wait_recv()
            value = part_slim[here].astype(F32)
            for i in range(PLANE - 1):
                value = value + into[i].astype(F32)
        for i in range(NZ):
            block[i] = value[PIECE * i : PIECE * (i + 1), :]
        z_wait = send_all(
            rz_sem.at[k],
            [(block.at[q], z_in.at[k, i], to) for i, (q, to) in enumerate(z_peers)],
            z_in.at[k],
        )

        gram_z_wait.wait_recv()
        value = gram_z[k, 0]
        for i in range(1, NZ):
            value = value + gram_z[k, i]
        gram[k, here] = value
        gram_all_wait = send_all(
            ga_sem.at[k],
            [(gram.at[k, here], gram.at[k, here], to) for _, to in plane_peers],
            gram.at[k, pl.ds(0, PLANE - 1)],
        )

        z_wait.wait_recv()
        value = block[z]
        for i in range(NZ - 1):
            value = value + z_in[k, i]
        z_all[k, z] = value
        z_all_wait = send_all(
            az_sem.at[k],
            [(z_all.at[k, z], z_all.at[k, z], to) for _, to in z_peers],
            z_all.at[k, pl.ds(0, NZ - 1)],
        )

        gram_all_wait.wait_recv()
        inverse_factor([gram[k, i] for i in range(PLANE)], y_t)
        y_value = y_t[...]

        z_all_wait.wait_recv()
        value = z_all[k].reshape(K, K)
        waits += [gram_wait, gram_z_wait, z_wait, gram_all_wait, z_all_wait]
        if wide:
            side_wide[x, y] = exact_dot(y_value, value)
            x_wait = send_all(
                wide_sem.at[4],
                [(side_wide.at[x, y, TOP], side_wide.at[x, y, TOP], to) for _, to in x_peers],
                side_wide.at[0, pl.ds(0, NX - 1), TOP],
            )
            y_wait = send_all(
                wide_sem.at[5],
                [(side_wide.at[x, y, LOW], side_wide.at[x, y, LOW], to) for _, to in y_peers],
                side_wide.at[0, pl.ds(0, NY - 1), LOW],
            )
            x_wait.wait_recv()
            xy_wait = send_all(
                wide_sem.at[6],
                [(side_wide.at[:, y, TOP], side_wide.at[:, y, TOP], to) for _, to in y_peers],
                side_wide.at[pl.ds(0, NY - 1), :, TOP],
            )
            y_wait.wait_recv()
            yx_wait = send_all(
                wide_sem.at[7],
                [(side_wide.at[x, :, LOW], side_wide.at[x, :, LOW], to) for _, to in x_peers],
                side_wide.at[pl.ds(0, NX - 1), :, LOW],
            )
            xy_wait.wait_recv()
            yx_wait.wait_recv()
            waits += [x_wait, y_wait, xy_wait, yx_wait]
        elif not last:
            whole = side_slim.at[k - 1]
            whole[here] = exact_dot(y_value, value).astype(BF16)
            all_wait = send_all(
                ap_sem.at[k],
                [(whole.at[here], whole.at[here], to) for _, to in plane_peers],
                whole.at[pl.ds(0, PLANE - 1)],
            )
            all_wait.wait_recv()
            waits += [all_wait]
        else:
            whole = side_slim.at[k - 1]
            whole[here] = exact_dot(value, y_value / SCALE, TN).astype(BF16)
            copies = [
                send(whole.at[here], whole.at[here], last_sem.at[0, i], last_sem.at[1, i], to)
                for i, (_, to) in enumerate(plane_peers)
            ]

            def pass_on(i, q):
                keep = pltpu.make_async_copy(whole.at[q], proj_out.at[core, q], fo_l.at[i])
                keep.start()
                to = proj_out.at[core, q]
                return [keep, send(whole.at[q], to, fo_s.at[i], fo_r.at[i], partner)]

            outs = pass_on(PLANE - 1, here)
            basis_out[...] = exact_dot(t_ref[core], y_value * SCALE, TN)
            for i in reversed(range(PLANE - 1)):
                copies[i].wait_recv()
                outs += pass_on(i, plane_source(PLANE_STEPS[i]))
            for copy in copies:
                copy.wait_send()
            for copy in outs:
                copy.wait()
        for wait in waits:
            wait.wait_send()
        if last:
            break

        pairs = []
        for j in range(PLANE // 2):
            if wide:
                p, q = j // 2, 2 * (j % 2)
                pair = jnp.concatenate([side_wide[p, q], side_wide[p, q + 1]], axis=1)
                pairs.append(jnp.concatenate(halves(pair), axis=0))
            else:
                pairs.append(jnp.concatenate([whole[2 * j], whole[2 * j + 1]], axis=1))
        split = jnp.concatenate(pairs, axis=1)
        total = lax.dot_general(split, split, NT, preferred_element_type=F32)
        if wide:
            total = total[:K] + total[K:]
            total = total[:, :K] + total[:, K:]
        sg_own[...] = total
        swap_gram = send(sg_own, sg_in.at[k], sg_sem.at[k, 0], sg_sem.at[k, 1], partner)
        for half in range(NC):
            value = lax.dot_general(split, a_tile[half], NT, preferred_element_type=F32)
            tp_own[half] = value[:K] + value[K:] if wide else value
        swap_part = send(tp_own, tp_in.at[k], tp_sem.at[k, 0], tp_sem.at[k, 1], partner)
        swap_gram.wait()
        total = sg_own[...] + sg_in[k]
        inverse_factor([total[8 * i : 8 * i + 8, :] for i in range(PLANE)], y_s)
        swap_part.wait()
        y_value = y_s[...]
        for half in range(NC):
            t_ref[half] = exact_dot(y_value, tp_own[half] + tp_in[k, half])


def sweep(embeddings, sketch):
    vmem = pl.BlockSpec(memory_space=pltpu.VMEM)
    hbm = pl.BlockSpec(memory_space=pl.ANY)
    dma = pltpu.SemaphoreType.DMA
    near, far = PLANE - 1, NZ - 1
    return pl.pallas_call(
        kernel,
        out_shape=(
            jax.ShapeDtypeStruct((NC, PLANE, K, K), BF16),
            jax.ShapeDtypeStruct((ROWS, K), F32),
        ),
        in_specs=[hbm, hbm],
        out_specs=(hbm, vmem),
        scratch_shapes=[
            pltpu.VMEM((NC, ROWS, HALF), BF16),
            pltpu.VMEM((ROWS, HALF), BF16),
            pltpu.VMEM((D, K), BF16),
            pltpu.VMEM((NC, K, ROWS), F32),
            pltpu.VMEM((NX, NY, K, K), F32),
            pltpu.VMEM((PLANE, K, K), BF16),
            pltpu.VMEM((NX - 1, NY, K // 2, K), F32),
            pltpu.VMEM((NY - 1, NX, K // 2, K), F32),
            pltpu.VMEM((NY, K // 2, K), F32),
            pltpu.VMEM((NX, K // 2, K), F32),
            pltpu.VMEM((NY - 1, K // 2, K), F32),
            pltpu.VMEM((NX - 1, K // 2, K), F32),
            pltpu.VMEM((ITERS, near, K, K), BF16),
            pltpu.VMEM((NZ, PIECE, K), F32),
            pltpu.VMEM((STEPS, far, PIECE, K), F32),
            pltpu.VMEM((STEPS, NZ, PIECE, K), F32),
            pltpu.VMEM((NX, NY, K, K), F32),
            pltpu.VMEM((ITERS, PLANE, K, K), BF16),
            pltpu.VMEM((PLANE, 8, K), F32),
            pltpu.VMEM((STEPS, near, 8, K), F32),
            pltpu.VMEM((STEPS, NZ, 8, K), F32),
            pltpu.VMEM((STEPS, PLANE, 8, K), F32),
            pltpu.VMEM((K, K), F32),
            pltpu.VMEM((K, K), F32),
            pltpu.VMEM((K, K), F32),
            pltpu.VMEM((ITERS, K, K), F32),
            pltpu.VMEM((NC, K, ROWS), F32),
            pltpu.VMEM((ITERS, NC, K, ROWS), F32),
            dma((3,)), dma((4,)), dma((8, 2)),
            dma((STEPS, 2)), dma((STEPS, 2)), dma((STEPS, 2)), dma((STEPS, 2)),
            dma((STEPS, 2)), dma((STEPS, 2)), dma((STEPS, 2)),
            dma((ITERS, 2)), dma((ITERS, 2)),
            dma((2, near)), dma((PLANE,)), dma((PLANE,)), dma((PLANE,)),
        ],
        compiler_params=pltpu.CompilerParams(
            collective_id=0, has_side_effects=True, vmem_limit_bytes=62 * 2**20
        ),
        name="sweep",
    )(embeddings, sketch)


def finish_kernel(proj_ref, basis_ref, basis_out, proj_out):
    proj_out[...] = proj_ref[...].astype(F32)
    basis_out[...] = basis_ref[...]


def finish(projected, basis):
    steps = 4
    tall = pl.BlockSpec((D // steps, K), lambda i: (i, 0))
    short = pl.BlockSpec((ROWS // steps, K), lambda i: (i, 0))
    return pl.pallas_call(
        finish_kernel,
        grid=(steps,),
        out_shape=(
            jax.ShapeDtypeStruct((ROWS, K), F32),
            jax.ShapeDtypeStruct((D, K), F32),
        ),
        in_specs=[tall, short],
        out_specs=(short, tall),
        name="finish",
    )(projected, basis)


def per_device(embeddings, sketch):
    projected, basis = sweep(embeddings, sketch)
    return finish(projected.reshape(D, K), basis)


def solution(mesh):
    return jax.shard_map(
        per_device,
        mesh=mesh,
        in_specs=(P(("grp", "row"), None), P()),
        out_specs=(P(("grp", "row"), None), P()),
        check_vma=False,
    )
```

```python
import math

import jax
import jax.numpy as jnp
from jax import lax
from jax.experimental import pallas as pl
from jax.experimental.pallas import tpu as pltpu
from jax.sharding import PartitionSpec as P

ITERS = 2
STEPS = ITERS + 1
K = 128
D = 4096
HALF = D // 2
ROWS = 256
NX, NY, NZ, NC = 4, 4, 8, 2
PLANE = NX * NY
PIECE = K // NZ
F32 = jnp.float32
BF16 = jnp.bfloat16
MESH = pl.DeviceIdType.MESH


def hops(step, size):
    return min(step, size - step)


RING = [2, 1, 3]
Z_STEPS = sorted(range(1, NZ), key=lambda c: -hops(c, NZ))
PLANE_STEPS = [(a, b) for a in RING + [0] for b in RING + [0] if (a, b) != (0, 0)]
SCALE = math.sqrt(ROWS * NX * NY * NZ * NC)
NT = (((1,), (1,)), ((), ()))
TN = (((0,), (1,)), ((), ()))
TOP, LOW = pl.ds(0, K // 2), pl.ds(K // 2, K // 2)


def exact_dot(a, b, dims=(((1,), (0,)), ((), ()))):
    return lax.dot_general(
        a, b, dims, precision=lax.Precision.HIGHEST, preferred_element_type=F32
    )


def halves(value):
    high = value.astype(BF16)
    low = (value - high.astype(F32)).astype(BF16)
    return high, low


def lane_copy(value, j):
    index = jnp.full(value.shape, j, jnp.int32)
    return jnp.take_along_axis(value, index, axis=1)


def row_copy(value, j):
    return jnp.broadcast_to(value[j : j + 1, :], value.shape)


def inverse_factor(gram, out_ref):
    sub = lax.broadcasted_iota(jnp.int32, (8, K), 0)
    lane = lax.broadcasted_iota(jnp.int32, (8, K), 1)
    blocks = K // 8
    diagonal = [jnp.where(lane == sub + 8 * i, gram[i], 0.0) for i in range(blocks)]
    total = diagonal[0]
    for i in range(1, blocks):
        total = total + diagonal[i]
    lanes = jnp.broadcast_to(lax.rsqrt(jnp.sum(total, axis=0, keepdims=True)), (8, K))
    y = [jnp.where(lane == sub + 8 * i, lanes, 0.0) for i in range(blocks)]
    g = [
        gram[i] * lanes * lax.rsqrt(jnp.sum(diagonal[i], axis=1, keepdims=True))
        for i in range(blocks)
    ]
    for b in range(blocks):
        columns = [lane_copy(g[b], 8 * b + j) for j in range(8)]
        upper, inverse, g_rows, y_rows = {}, [], [], []
        scale = jnp.zeros((8, K), F32)
        for j in range(0, 8, 2):
            first, cross = row_copy(columns[j], j), row_copy(columns[j + 1], j)
            second = row_copy(columns[j + 1], j + 1)
            minor = first * second - cross * cross
            inverse += [1.0 / first, first * (1.0 / minor)]
            upper[j, j + 1] = cross
            scale = jnp.where(sub == j, lax.rsqrt(first), scale)
            scale = jnp.where(sub == j + 1, lax.rsqrt(minor * inverse[j]), scale)
            f0 = jnp.where(sub > j, columns[j], 0.0) * inverse[j]
            f1 = jnp.where(sub > j + 1, columns[j + 1] - f0 * cross, 0.0) * inverse[j + 1]
            g_rows.append(row_copy(g[b], j))
            y_rows.append(row_copy(y[b], j))
            g_next = g[b] - f0 * g_rows[j]
            y_next = y[b] - f0 * y_rows[j]
            g_rows.append(row_copy(g_next, j + 1))
            y_rows.append(row_copy(y_next, j + 1))
            g[b] = g_next - f1 * g_rows[j + 1]
            y[b] = y_next - f1 * y_rows[j + 1]
            for m in range(j + 2, 8):
                upper[j, m] = row_copy(columns[m], j)
                column = columns[m] - f0 * upper[j, m]
                upper[j + 1, m] = row_copy(column, j + 1)
                columns[m] = column - f1 * upper[j + 1, m]
        for i in range(b + 1, blocks):
            factors = []
            gi, yi = g[i], y[i]
            for j in range(8):
                column = lane_copy(g[i], 8 * b + j)
                for m in range(j):
                    column = column - factors[m] * upper[m, j]
                factors.append(column * inverse[j])
                gi = gi - factors[j] * g_rows[j]
                yi = yi - factors[j] * y_rows[j]
            g[i], y[i] = gi, yi
        out_ref[8 * b : 8 * b + 8, :] = y[b] * scale


def kernel(
    a_hbm, s_hbm, proj_out, basis_out,
    a_tile, a_rest, s_all, t_ref, part_wide, part_slim, in_x, in_y, sum_x, sum_y, in_xy,
    in_yx, in_slim, block, z_in, z_all, side_wide, side_slim, gram_part, gram_in, gram_z,
    gram, y_t, y_s, sg_own, sg_in, tp_own, tp_in,
    local_sem, swap_sem, wide_sem, rp_sem, rz_sem, az_sem, ap_sem, gp_sem, gz_sem, ga_sem,
    sg_sem, tp_sem, last_sem, fo_s, fo_r, fo_l,
):
    y = lax.axis_index("grp")
    row = lax.axis_index("row")
    x, z, core = row // (NZ * NC), (row // NC) % NZ, row % NC
    other = 1 - core
    here = x * NY + y

    def at(x_to, y_to, z_to, core_to):
        return (y_to, (x_to * NZ + z_to) * NC + core_to)

    def plane_peer(step):
        x_to, y_to = (x + step[0]) % NX, (y + step[1]) % NY
        return x_to * NY + y_to, at(x_to, y_to, z, core)

    def plane_source(step):
        return (x - step[0]) % NX * NY + (y - step[1]) % NY

    def z_peer(step):
        z_to = (z + step) % NZ
        return z_to, at(x, y, z_to, core)

    partner = at(x, y, z, other)
    plane_peers = [plane_peer(step) for step in PLANE_STEPS]
    z_peers = [z_peer(step) for step in Z_STEPS]
    x_peers = [((x + step) % NX, at((x + step) % NX, y, z, core)) for step in RING]
    y_peers = [((y + step) % NY, at(x, (y + step) % NY, z, core)) for step in RING]

    def send(src, dst, send_sem, recv_sem, device):
        copy = pltpu.make_async_remote_copy(
            src, dst, send_sem, recv_sem, device_id=device, device_id_type=MESH
        )
        copy.start()
        return copy

    def send_all(sem, copies, size):
        for src, dst, device in copies:
            send(src, dst, sem.at[0], sem.at[1], device)
        return pltpu.make_async_remote_copy(
            size, size, sem.at[0], sem.at[1], device_id=partner, device_id_type=MESH
        )

    own_half = pl.ds(pl.multiple_of(core * HALF, HALF), HALF)
    other_half = pl.ds(pl.multiple_of(other * HALF, HALF), HALF)
    loads = [
        pltpu.make_async_copy(a_hbm.at[:, own_half], a_tile.at[core], local_sem.at[0]),
        pltpu.make_async_copy(a_hbm.at[:, other_half], a_rest, local_sem.at[1]),
        pltpu.make_async_copy(s_hbm, s_all, local_sem.at[2]),
    ]
    for copy in loads:
        copy.start()

    barrier = pltpu.get_barrier_semaphore()
    everyone = [device for _, device in plane_peers + z_peers] + [partner]
    for device in everyone:
        pl.semaphore_signal(barrier, inc=1, device_id=device, device_id_type=MESH)
    for copy in loads:
        copy.wait()
    first = jnp.dot(a_tile[core], s_all[own_half, :], preferred_element_type=F32)
    first = first + jnp.dot(a_rest[...], s_all[other_half, :], preferred_element_type=F32)
    t_ref[core] = first.T
    pl.semaphore_wait(barrier, len(everyone))

    swap_t = send(t_ref.at[core], t_ref.at[core], swap_sem.at[0], swap_sem.at[1], partner)
    swap_a = send(a_rest, a_tile.at[core], swap_sem.at[2], swap_sem.at[3], partner)
    swap_t.wait()

    for k in range(STEPS):
        wide, last = k == 0, k == ITERS
        waits = []

        t0, t1 = t_ref[0], t_ref[1]
        local = exact_dot(t0, t0, NT) + exact_dot(t1, t1, NT)
        for i in range(PLANE):
            gram_part[i] = local[8 * i : 8 * i + 8, :]
        gram_wait = send_all(
            gp_sem.at[k],
            [(gram_part.at[q], gram_in.at[k, i], to) for i, (q, to) in enumerate(plane_peers)],
            gram_in.at[k],
        )

        if wide:
            swap_a.wait()
        t0_split = jnp.concatenate(halves(t0), axis=0)
        t1_split = jnp.concatenate(halves(t1), axis=0)
        for j in range(PLANE // 2):
            columns = slice(2 * K * j, 2 * K * (j + 1))
            value = jnp.dot(t0_split, a_tile[0, :, columns], preferred_element_type=F32)
            value = value + jnp.dot(t1_split, a_tile[1, :, columns], preferred_element_type=F32)
            value = value[:K] + value[K:]
            for i in range(2):
                q, part = 2 * j + i, value[:, K * i : K * (i + 1)]
                if wide:
                    part_wide[q // NY, q % NY] = part
                else:
                    part_slim[q] = part.astype(BF16)
        if wide:
            x_wait = send_all(
                wide_sem.at[0],
                [(part_wide.at[q, :, TOP], in_x.at[i], to) for i, (q, to) in enumerate(x_peers)],
                in_x,
            )
            y_wait = send_all(
                wide_sem.at[1],
                [(part_wide.at[:, q, LOW], in_y.at[i], to) for i, (q, to) in enumerate(y_peers)],
                in_y,
            )
            waits += [x_wait, y_wait]
        else:
            into = in_slim.at[k - 1]
            side_wait = send_all(
                rp_sem.at[k],
                [(part_slim.at[q], into.at[i], to) for i, (q, to) in enumerate(plane_peers)],
                into,
            )
            waits += [side_wait]

        gram_wait.wait_recv()
        value = gram_part[here]
        for i in range(PLANE - 1):
            value = value + gram_in[k, i]
        gram_z[k, z] = value
        gram_z_wait = send_all(
            gz_sem.at[k],
            [(gram_z.at[k, z], gram_z.at[k, z], to) for _, to in z_peers],
            gram_z.at[k, pl.ds(0, NZ - 1)],
        )

        if wide:
            x_wait.wait_recv()
            value = part_wide[x, :, TOP]
            for i in range(NX - 1):
                value = value + in_x[i]
            sum_x[...] = value
            xy_wait = send_all(
                wide_sem.at[2],
                [(sum_x.at[q], in_xy.at[i], to) for i, (q, to) in enumerate(y_peers)],
                in_xy,
            )
            y_wait.wait_recv()
            value = part_wide[:, y, LOW]
            for i in range(NY - 1):
                value = value + in_y[i]
            sum_y[...] = value
            yx_wait = send_all(
                wide_sem.at[3],
                [(sum_y.at[q], in_yx.at[i], to) for i, (q, to) in enumerate(x_peers)],
                in_yx,
            )
            xy_wait.wait_recv()
            top = sum_x[y]
            for i in range(NY - 1):
                top = top + in_xy[i]
            yx_wait.wait_recv()
            low = sum_y[x]
            for i in range(NX - 1):
                low = low + in_yx[i]
            value = jnp.concatenate([top, low], axis=0)
            waits += [xy_wait, yx_wait]
        else:
            side_wait.wait_recv()
            value = part_slim[here].astype(F32)
            for i in range(PLANE - 1):
                value = value + into[i].astype(F32)
        for i in range(NZ):
            block[i] = value[PIECE * i : PIECE * (i + 1), :]
        z_wait = send_all(
            rz_sem.at[k],
            [(block.at[q], z_in.at[k, i], to) for i, (q, to) in enumerate(z_peers)],
            z_in.at[k],
        )

        gram_z_wait.wait_recv()
        value = gram_z[k, 0]
        for i in range(1, NZ):
            value = value + gram_z[k, i]
        gram[k, here] = value
        gram_all_wait = send_all(
            ga_sem.at[k],
            [(gram.at[k, here], gram.at[k, here], to) for _, to in plane_peers],
            gram.at[k, pl.ds(0, PLANE - 1)],
        )

        z_wait.wait_recv()
        value = block[z]
        for i in range(NZ - 1):
            value = value + z_in[k, i]
        z_all[k, z] = value
        z_all_wait = send_all(
            az_sem.at[k],
            [(z_all.at[k, z], z_all.at[k, z], to) for _, to in z_peers],
            z_all.at[k, pl.ds(0, NZ - 1)],
        )

        gram_all_wait.wait_recv()
        inverse_factor([gram[k, i] for i in range(PLANE)], y_t)
        y_value = y_t[...]

        z_all_wait.wait_recv()
        value = z_all[k].reshape(K, K)
        waits += [gram_wait, gram_z_wait, z_wait, gram_all_wait, z_all_wait]
        if wide:
            side_wide[x, y] = exact_dot(y_value, value)
            x_wait = send_all(
                wide_sem.at[4],
                [(side_wide.at[x, y, TOP], side_wide.at[x, y, TOP], to) for _, to in x_peers],
                side_wide.at[0, pl.ds(0, NX - 1), TOP],
            )
            y_wait = send_all(
                wide_sem.at[5],
                [(side_wide.at[x, y, LOW], side_wide.at[x, y, LOW], to) for _, to in y_peers],
                side_wide.at[0, pl.ds(0, NY - 1), LOW],
            )
            x_wait.wait_recv()
            xy_wait = send_all(
                wide_sem.at[6],
                [(side_wide.at[:, y, TOP], side_wide.at[:, y, TOP], to) for _, to in y_peers],
                side_wide.at[pl.ds(0, NY - 1), :, TOP],
            )
            y_wait.wait_recv()
            yx_wait = send_all(
                wide_sem.at[7],
                [(side_wide.at[x, :, LOW], side_wide.at[x, :, LOW], to) for _, to in x_peers],
                side_wide.at[pl.ds(0, NX - 1), :, LOW],
            )
            xy_wait.wait_recv()
            yx_wait.wait_recv()
            waits += [x_wait, y_wait, xy_wait, yx_wait]
        elif not last:
            whole = side_slim.at[k - 1]
            whole[here] = exact_dot(y_value, value).astype(BF16)
            all_wait = send_all(
                ap_sem.at[k],
                [(whole.at[here], whole.at[here], to) for _, to in plane_peers],
                whole.at[pl.ds(0, PLANE - 1)],
            )
            all_wait.wait_recv()
            waits += [all_wait]
        else:
            whole = side_slim.at[k - 1]
            whole[here] = exact_dot(value, y_value / SCALE, TN).astype(BF16)
            copies = [
                send(whole.at[here], whole.at[here], last_sem.at[0, i], last_sem.at[1, i], to)
                for i, (_, to) in enumerate(plane_peers)
            ]

            def pass_on(i, q):
                keep = pltpu.make_async_copy(whole.at[q], proj_out.at[core, q], fo_l.at[i])
                keep.start()
                to = proj_out.at[core, q]
                return [keep, send(whole.at[q], to, fo_s.at[i], fo_r.at[i], partner)]

            outs = pass_on(PLANE - 1, here)
            basis_out[...] = exact_dot(t_ref[core], y_value * SCALE, TN)
            for i in reversed(range(PLANE - 1)):
                copies[i].wait_recv()
                outs += pass_on(i, plane_source(PLANE_STEPS[i]))
            for copy in copies:
                copy.wait_send()
            for copy in outs:
                copy.wait()
        if last:
            for wait in waits:
                wait.wait_send()
            break

        pairs = []
        for j in range(PLANE // 2):
            if wide:
                p, q = j // 2, 2 * (j % 2)
                pair = jnp.concatenate([side_wide[p, q], side_wide[p, q + 1]], axis=1)
                pairs.append(jnp.concatenate(halves(pair), axis=0))
            else:
                pairs.append(jnp.concatenate([whole[2 * j], whole[2 * j + 1]], axis=1))
        split = jnp.concatenate(pairs, axis=1)
        total = lax.dot_general(split, split, NT, preferred_element_type=F32)
        if wide:
            total = total[:K] + total[K:]
            total = total[:, :K] + total[:, K:]
        sg_own[...] = total
        swap_gram = send(sg_own, sg_in.at[k], sg_sem.at[k, 0], sg_sem.at[k, 1], partner)
        for half in range(NC):
            value = lax.dot_general(split, a_tile[half], NT, preferred_element_type=F32)
            tp_own[half] = value[:K] + value[K:] if wide else value
        swap_part = send(tp_own, tp_in.at[k], tp_sem.at[k, 0], tp_sem.at[k, 1], partner)
        swap_gram.wait()
        total = sg_own[...] + sg_in[k]
        inverse_factor([total[8 * i : 8 * i + 8, :] for i in range(PLANE)], y_s)
        swap_part.wait()
        y_value = y_s[...]
        for half in range(NC):
            t_ref[half] = exact_dot(y_value, tp_own[half] + tp_in[k, half])
        for wait in waits:
            wait.wait_send()


def sweep(embeddings, sketch):
    vmem = pl.BlockSpec(memory_space=pltpu.VMEM)
    hbm = pl.BlockSpec(memory_space=pl.ANY)
    dma = pltpu.SemaphoreType.DMA
    near, far = PLANE - 1, NZ - 1
    return pl.pallas_call(
        kernel,
        out_shape=(
            jax.ShapeDtypeStruct((NC, PLANE, K, K), BF16),
            jax.ShapeDtypeStruct((ROWS, K), F32),
        ),
        in_specs=[hbm, hbm],
        out_specs=(hbm, vmem),
        scratch_shapes=[
            pltpu.VMEM((NC, ROWS, HALF), BF16),
            pltpu.VMEM((ROWS, HALF), BF16),
            pltpu.VMEM((D, K), BF16),
            pltpu.VMEM((NC, K, ROWS), F32),
            pltpu.VMEM((NX, NY, K, K), F32),
            pltpu.VMEM((PLANE, K, K), BF16),
            pltpu.VMEM((NX - 1, NY, K // 2, K), F32),
            pltpu.VMEM((NY - 1, NX, K // 2, K), F32),
            pltpu.VMEM((NY, K // 2, K), F32),
            pltpu.VMEM((NX, K // 2, K), F32),
            pltpu.VMEM((NY - 1, K // 2, K), F32),
            pltpu.VMEM((NX - 1, K // 2, K), F32),
            pltpu.VMEM((ITERS, near, K, K), BF16),
            pltpu.VMEM((NZ, PIECE, K), F32),
            pltpu.VMEM((STEPS, far, PIECE, K), F32),
            pltpu.VMEM((STEPS, NZ, PIECE, K), F32),
            pltpu.VMEM((NX, NY, K, K), F32),
            pltpu.VMEM((ITERS, PLANE, K, K), BF16),
            pltpu.VMEM((PLANE, 8, K), F32),
            pltpu.VMEM((STEPS, near, 8, K), F32),
            pltpu.VMEM((STEPS, NZ, 8, K), F32),
            pltpu.VMEM((STEPS, PLANE, 8, K), F32),
            pltpu.VMEM((K, K), F32),
            pltpu.VMEM((K, K), F32),
            pltpu.VMEM((K, K), F32),
            pltpu.VMEM((ITERS, K, K), F32),
            pltpu.VMEM((NC, K, ROWS), F32),
            pltpu.VMEM((ITERS, NC, K, ROWS), F32),
            dma((3,)), dma((4,)), dma((8, 2)),
            dma((STEPS, 2)), dma((STEPS, 2)), dma((STEPS, 2)), dma((STEPS, 2)),
            dma((STEPS, 2)), dma((STEPS, 2)), dma((STEPS, 2)),
            dma((ITERS, 2)), dma((ITERS, 2)),
            dma((2, near)), dma((PLANE,)), dma((PLANE,)), dma((PLANE,)),
        ],
        compiler_params=pltpu.CompilerParams(
            collective_id=0, has_side_effects=True, vmem_limit_bytes=62 * 2**20
        ),
        name="sweep",
    )(embeddings, sketch)


def finish_kernel(proj_ref, basis_ref, basis_out, proj_out):
    proj_out[...] = proj_ref[...].astype(F32)
    basis_out[...] = basis_ref[...]


def finish(projected, basis):
    steps = 2
    tall = pl.BlockSpec((D // steps, K), lambda i: (i, 0))
    short = pl.BlockSpec((ROWS // steps, K), lambda i: (i, 0))
    return pl.pallas_call(
        finish_kernel,
        grid=(steps,),
        out_shape=(
            jax.ShapeDtypeStruct((ROWS, K), F32),
            jax.ShapeDtypeStruct((D, K), F32),
        ),
        in_specs=[tall, short],
        out_specs=(short, tall),
        name="finish",
    )(projected, basis)


def per_device(embeddings, sketch):
    projected, basis = sweep(embeddings, sketch)
    return finish(projected.reshape(D, K), basis)


def solution(mesh):
    return jax.shard_map(
        per_device,
        mesh=mesh,
        in_specs=(P(("grp", "row"), None), P()),
        out_specs=(P(("grp", "row"), None), P()),
        check_vma=False,
    )
```

```python
import math

import jax
import jax.numpy as jnp
from jax import lax
from jax.experimental import pallas as pl
from jax.experimental.pallas import tpu as pltpu
from jax.sharding import PartitionSpec as P

ITERS = 2
STEPS = ITERS + 1
K = 128
D = 4096
HALF = D // 2
ROWS = 256
NX, NY, NZ, NC = 4, 4, 8, 2
PLANE = NX * NY
PIECE = K // NZ
F32 = jnp.float32
BF16 = jnp.bfloat16
MESH = pl.DeviceIdType.MESH


def hops(step, size):
    return min(step, size - step)


RING = [2, 1, 3]
Z_STEPS = sorted(range(1, NZ), key=lambda c: -hops(c, NZ))
PLANE_STEPS = [(a, b) for a in RING + [0] for b in RING + [0] if (a, b) != (0, 0)]
SCALE = math.sqrt(ROWS * NX * NY * NZ * NC)
NT = (((1,), (1,)), ((), ()))
TN = (((0,), (1,)), ((), ()))
TOP, LOW = pl.ds(0, K // 2), pl.ds(K // 2, K // 2)


def exact_dot(a, b, dims=(((1,), (0,)), ((), ()))):
    return lax.dot_general(
        a, b, dims, precision=lax.Precision.HIGHEST, preferred_element_type=F32
    )


def halves(value):
    high = value.astype(BF16)
    low = (value - high.astype(F32)).astype(BF16)
    return high, low


def lane_copy(value, j):
    index = jnp.full(value.shape, j, jnp.int32)
    return jnp.take_along_axis(value, index, axis=1)


def row_copy(value, j):
    return jnp.broadcast_to(value[j : j + 1, :], value.shape)


def inverse_factor(gram, out_ref):
    sub = lax.broadcasted_iota(jnp.int32, (8, K), 0)
    lane = lax.broadcasted_iota(jnp.int32, (8, K), 1)
    blocks = K // 8
    diagonal = [jnp.where(lane == sub + 8 * i, gram[i], 0.0) for i in range(blocks)]
    total = diagonal[0]
    for i in range(1, blocks):
        total = total + diagonal[i]
    lanes = jnp.broadcast_to(lax.rsqrt(jnp.sum(total, axis=0, keepdims=True)), (8, K))
    y = [jnp.where(lane == sub + 8 * i, lanes, 0.0) for i in range(blocks)]
    g = [
        gram[i] * lanes * lax.rsqrt(jnp.sum(diagonal[i], axis=1, keepdims=True))
        for i in range(blocks)
    ]
    for b in range(blocks):
        columns = [lane_copy(g[b], 8 * b + j) for j in range(8)]
        upper, inverse, g_rows, y_rows = {}, [], [], []
        scale = jnp.zeros((8, K), F32)
        for j in range(0, 8, 2):
            first, cross = row_copy(columns[j], j), row_copy(columns[j + 1], j)
            second = row_copy(columns[j + 1], j + 1)
            minor = first * second - cross * cross
            inverse += [1.0 / first, first * (1.0 / minor)]
            upper[j, j + 1] = cross
            scale = jnp.where(sub == j, lax.rsqrt(first), scale)
            scale = jnp.where(sub == j + 1, lax.rsqrt(minor * inverse[j]), scale)
            f0 = jnp.where(sub > j, columns[j], 0.0) * inverse[j]
            f1 = jnp.where(sub > j + 1, columns[j + 1] - f0 * cross, 0.0) * inverse[j + 1]
            g_rows.append(row_copy(g[b], j))
            y_rows.append(row_copy(y[b], j))
            g_next = g[b] - f0 * g_rows[j]
            y_next = y[b] - f0 * y_rows[j]
            g_rows.append(row_copy(g_next, j + 1))
            y_rows.append(row_copy(y_next, j + 1))
            g[b] = g_next - f1 * g_rows[j + 1]
            y[b] = y_next - f1 * y_rows[j + 1]
            for m in range(j + 2, 8):
                upper[j, m] = row_copy(columns[m], j)
                column = columns[m] - f0 * upper[j, m]
                upper[j + 1, m] = row_copy(column, j + 1)
                columns[m] = column - f1 * upper[j + 1, m]
        for i in range(b + 1, blocks):
            factors = []
            gi, yi = g[i], y[i]
            for j in range(8):
                column = lane_copy(g[i], 8 * b + j)
                for m in range(j):
                    column = column - factors[m] * upper[m, j]
                factors.append(column * inverse[j])
                gi = gi - factors[j] * g_rows[j]
                yi = yi - factors[j] * y_rows[j]
            g[i], y[i] = gi, yi
        out_ref[8 * b : 8 * b + 8, :] = y[b] * scale


def kernel(
    a_hbm, s_hbm, proj_out, basis_out,
    a_tile, a_rest, s_all, t_ref, part_wide, part_slim, in_x, in_y, sum_x, sum_y, in_xy,
    in_yx, in_slim, block, z_in, z_all, side_wide, side_slim, gram_part, gram_in, gram_z,
    gram, y_t, y_s, sg_own, sg_in, tp_own, tp_in,
    local_sem, swap_sem, wide_sem, rp_sem, rz_sem, az_sem, ap_sem, gp_sem, gz_sem, ga_sem,
    sg_sem, tp_sem, last_sem, fo_s, fo_r, fo_l,
):
    y = lax.axis_index("grp")
    row = lax.axis_index("row")
    x, z, core = row // (NZ * NC), (row // NC) % NZ, row % NC
    other = 1 - core
    here = x * NY + y

    def at(x_to, y_to, z_to, core_to):
        return (y_to, (x_to * NZ + z_to) * NC + core_to)

    def plane_peer(step):
        x_to, y_to = (x + step[0]) % NX, (y + step[1]) % NY
        return x_to * NY + y_to, at(x_to, y_to, z, core)

    def plane_source(step):
        return (x - step[0]) % NX * NY + (y - step[1]) % NY

    def z_peer(step):
        z_to = (z + step) % NZ
        return z_to, at(x, y, z_to, core)

    partner = at(x, y, z, other)
    plane_peers = [plane_peer(step) for step in PLANE_STEPS]
    z_peers = [z_peer(step) for step in Z_STEPS]
    x_peers = [((x + step) % NX, at((x + step) % NX, y, z, core)) for step in RING]
    y_peers = [((y + step) % NY, at(x, (y + step) % NY, z, core)) for step in RING]

    def send(src, dst, send_sem, recv_sem, device):
        copy = pltpu.make_async_remote_copy(
            src, dst, send_sem, recv_sem, device_id=device, device_id_type=MESH
        )
        copy.start()
        return copy

    def send_all(sem, copies, size):
        for src, dst, device in copies:
            send(src, dst, sem.at[0], sem.at[1], device)
        return pltpu.make_async_remote_copy(
            size, size, sem.at[0], sem.at[1], device_id=partner, device_id_type=MESH
        )

    own_half = pl.ds(pl.multiple_of(core * HALF, HALF), HALF)
    other_half = pl.ds(pl.multiple_of(other * HALF, HALF), HALF)
    loads = [
        pltpu.make_async_copy(a_hbm.at[:, own_half], a_tile.at[core], local_sem.at[0]),
        pltpu.make_async_copy(a_hbm.at[:, other_half], a_rest, local_sem.at[1]),
        pltpu.make_async_copy(s_hbm, s_all, local_sem.at[2]),
    ]
    barrier = pltpu.get_barrier_semaphore()
    everyone = [device for _, device in plane_peers + z_peers] + [partner]
    for device in everyone:
        pl.semaphore_signal(barrier, inc=1, device_id=device, device_id_type=MESH)
    for copy in loads:
        copy.start()
    for copy in loads:
        copy.wait()
    first = jnp.dot(a_tile[core], s_all[own_half, :], preferred_element_type=F32)
    first = first + jnp.dot(a_rest[...], s_all[other_half, :], preferred_element_type=F32)
    t_ref[core] = first.T
    pl.semaphore_wait(barrier, len(everyone))

    swap_t = send(t_ref.at[core], t_ref.at[core], swap_sem.at[0], swap_sem.at[1], partner)
    swap_a = send(a_rest, a_tile.at[core], swap_sem.at[2], swap_sem.at[3], partner)
    swap_t.wait()

    for k in range(STEPS):
        wide, last = k == 0, k == ITERS
        waits = []

        t0, t1 = t_ref[0], t_ref[1]
        local = exact_dot(t0, t0, NT) + exact_dot(t1, t1, NT)
        for i in range(PLANE):
            gram_part[i] = local[8 * i : 8 * i + 8, :]
        gram_wait = send_all(
            gp_sem.at[k],
            [(gram_part.at[q], gram_in.at[k, i], to) for i, (q, to) in enumerate(plane_peers)],
            gram_in.at[k],
        )

        if wide:
            mine = jnp.concatenate(halves(t_ref[core]), axis=0)
            theirs = jnp.concatenate(halves(t_ref[other]), axis=0)
            for j in range(PLANE // 2):
                columns = slice(2 * K * j, 2 * K * (j + 1))
                value = jnp.dot(mine, a_tile[core, :, columns], preferred_element_type=F32)
                value = value[:K] + value[K:]
                for i in range(2):
                    q = 2 * j + i
                    part_wide[q // NY, q % NY] = value[:, K * i : K * (i + 1)]
            swap_a.wait()
            for j in range(PLANE // 2):
                columns = slice(2 * K * j, 2 * K * (j + 1))
                value = jnp.dot(theirs, a_tile[other, :, columns], preferred_element_type=F32)
                value = value[:K] + value[K:]
                for i in range(2):
                    q = 2 * j + i
                    part_wide[q // NY, q % NY] += value[:, K * i : K * (i + 1)]
        else:
            t0_split = jnp.concatenate(halves(t0), axis=0)
            t1_split = jnp.concatenate(halves(t1), axis=0)
            for j in range(PLANE // 2):
                columns = slice(2 * K * j, 2 * K * (j + 1))
                value = jnp.dot(t0_split, a_tile[0, :, columns], preferred_element_type=F32)
                value = value + jnp.dot(
                    t1_split, a_tile[1, :, columns], preferred_element_type=F32
                )
                value = value[:K] + value[K:]
                for i in range(2):
                    part_slim[2 * j + i] = value[:, K * i : K * (i + 1)].astype(BF16)
        if wide:
            x_wait = send_all(
                wide_sem.at[0],
                [(part_wide.at[q, :, TOP], in_x.at[i], to) for i, (q, to) in enumerate(x_peers)],
                in_x,
            )
            y_wait = send_all(
                wide_sem.at[1],
                [(part_wide.at[:, q, LOW], in_y.at[i], to) for i, (q, to) in enumerate(y_peers)],
                in_y,
            )
            waits += [x_wait, y_wait]
        else:
            into = in_slim.at[k - 1]
            side_wait = send_all(
                rp_sem.at[k],
                [(part_slim.at[q], into.at[i], to) for i, (q, to) in enumerate(plane_peers)],
                into,
            )
            waits += [side_wait]

        gram_wait.wait_recv()
        value = gram_part[here]
        for i in range(PLANE - 1):
            value = value + gram_in[k, i]
        gram_z[k, z] = value
        gram_z_wait = send_all(
            gz_sem.at[k],
            [(gram_z.at[k, z], gram_z.at[k, z], to) for _, to in z_peers],
            gram_z.at[k, pl.ds(0, NZ - 1)],
        )

        if wide:
            x_wait.wait_recv()
            value = part_wide[x, :, TOP]
            for i in range(NX - 1):
                value = value + in_x[i]
            sum_x[...] = value
            xy_wait = send_all(
                wide_sem.at[2],
                [(sum_x.at[q], in_xy.at[i], to) for i, (q, to) in enumerate(y_peers)],
                in_xy,
            )
            y_wait.wait_recv()
            value = part_wide[:, y, LOW]
            for i in range(NY - 1):
                value = value + in_y[i]
            sum_y[...] = value
            yx_wait = send_all(
                wide_sem.at[3],
                [(sum_y.at[q], in_yx.at[i], to) for i, (q, to) in enumerate(x_peers)],
                in_yx,
            )
            xy_wait.wait_recv()
            top = sum_x[y]
            for i in range(NY - 1):
                top = top + in_xy[i]
            yx_wait.wait_recv()
            low = sum_y[x]
            for i in range(NX - 1):
                low = low + in_yx[i]
            value = jnp.concatenate([top, low], axis=0)
            waits += [xy_wait, yx_wait]
        else:
            side_wait.wait_recv()
            value = part_slim[here].astype(F32)
            for i in range(PLANE - 1):
                value = value + into[i].astype(F32)
        for i in range(NZ):
            block[i] = value[PIECE * i : PIECE * (i + 1), :]
        z_wait = send_all(
            rz_sem.at[k],
            [(block.at[q], z_in.at[k, i], to) for i, (q, to) in enumerate(z_peers)],
            z_in.at[k],
        )

        gram_z_wait.wait_recv()
        value = gram_z[k, 0]
        for i in range(1, NZ):
            value = value + gram_z[k, i]
        gram[k, here] = value
        gram_all_wait = send_all(
            ga_sem.at[k],
            [(gram.at[k, here], gram.at[k, here], to) for _, to in plane_peers],
            gram.at[k, pl.ds(0, PLANE - 1)],
        )

        z_wait.wait_recv()
        value = block[z]
        for i in range(NZ - 1):
            value = value + z_in[k, i]
        z_all[k, z] = value
        z_all_wait = send_all(
            az_sem.at[k],
            [(z_all.at[k, z], z_all.at[k, z], to) for _, to in z_peers],
            z_all.at[k, pl.ds(0, NZ - 1)],
        )

        gram_all_wait.wait_recv()
        inverse_factor([gram[k, i] for i in range(PLANE)], y_t)
        y_value = y_t[...]

        z_all_wait.wait_recv()
        value = z_all[k].reshape(K, K)
        waits += [gram_wait, gram_z_wait, z_wait, gram_all_wait, z_all_wait]
        if wide:
            side_wide[x, y] = exact_dot(y_value, value)
            x_wait = send_all(
                wide_sem.at[4],
                [(side_wide.at[x, y, TOP], side_wide.at[x, y, TOP], to) for _, to in x_peers],
                side_wide.at[0, pl.ds(0, NX - 1), TOP],
            )
            y_wait = send_all(
                wide_sem.at[5],
                [(side_wide.at[x, y, LOW], side_wide.at[x, y, LOW], to) for _, to in y_peers],
                side_wide.at[0, pl.ds(0, NY - 1), LOW],
            )
            x_wait.wait_recv()
            xy_wait = send_all(
                wide_sem.at[6],
                [(side_wide.at[:, y, TOP], side_wide.at[:, y, TOP], to) for _, to in y_peers],
                side_wide.at[pl.ds(0, NY - 1), :, TOP],
            )
            y_wait.wait_recv()
            yx_wait = send_all(
                wide_sem.at[7],
                [(side_wide.at[x, :, LOW], side_wide.at[x, :, LOW], to) for _, to in x_peers],
                side_wide.at[pl.ds(0, NX - 1), :, LOW],
            )
            xy_wait.wait_recv()
            yx_wait.wait_recv()
            waits += [x_wait, y_wait, xy_wait, yx_wait]
        elif not last:
            whole = side_slim.at[k - 1]
            whole[here] = exact_dot(y_value, value).astype(BF16)
            all_wait = send_all(
                ap_sem.at[k],
                [(whole.at[here], whole.at[here], to) for _, to in plane_peers],
                whole.at[pl.ds(0, PLANE - 1)],
            )
            all_wait.wait_recv()
            waits += [all_wait]
        else:
            whole = side_slim.at[k - 1]
            whole[here] = exact_dot(value, y_value / SCALE, TN).astype(BF16)
            copies = [
                send(whole.at[here], whole.at[here], last_sem.at[0, i], last_sem.at[1, i], to)
                for i, (_, to) in enumerate(plane_peers)
            ]

            def pass_on(i, q):
                keep = pltpu.make_async_copy(whole.at[q], proj_out.at[core, q], fo_l.at[i])
                keep.start()
                to = proj_out.at[core, q]
                return [keep, send(whole.at[q], to, fo_s.at[i], fo_r.at[i], partner)]

            outs = pass_on(PLANE - 1, here)
            basis_out[...] = exact_dot(t_ref[core], y_value * SCALE, TN)
            for i in reversed(range(PLANE - 1)):
                copies[i].wait_recv()
                outs += pass_on(i, plane_source(PLANE_STEPS[i]))
            for copy in copies:
                copy.wait_send()
            for copy in outs:
                copy.wait()
        if last:
            for wait in waits:
                wait.wait_send()
            break

        pairs = []
        for j in range(PLANE // 2):
            if wide:
                p, q = j // 2, 2 * (j % 2)
                pair = jnp.concatenate([side_wide[p, q], side_wide[p, q + 1]], axis=1)
                pairs.append(jnp.concatenate(halves(pair), axis=0))
            else:
                pairs.append(jnp.concatenate([whole[2 * j], whole[2 * j + 1]], axis=1))
        split = jnp.concatenate(pairs, axis=1)
        total = lax.dot_general(split, split, NT, preferred_element_type=F32)
        if wide:
            total = total[:K] + total[K:]
            total = total[:, :K] + total[:, K:]
        sg_own[...] = total
        swap_gram = send(sg_own, sg_in.at[k], sg_sem.at[k, 0], sg_sem.at[k, 1], partner)
        for half in range(NC):
            value = lax.dot_general(split, a_tile[half], NT, preferred_element_type=F32)
            tp_own[half] = value[:K] + value[K:] if wide else value
        swap_part = send(tp_own, tp_in.at[k], tp_sem.at[k, 0], tp_sem.at[k, 1], partner)
        swap_gram.wait()
        total = sg_own[...] + sg_in[k]
        inverse_factor([total[8 * i : 8 * i + 8, :] for i in range(PLANE)], y_s)
        swap_part.wait()
        y_value = y_s[...]
        for half in range(NC):
            t_ref[half] = exact_dot(y_value, tp_own[half] + tp_in[k, half])
        for wait in waits:
            wait.wait_send()


def sweep(embeddings, sketch):
    vmem = pl.BlockSpec(memory_space=pltpu.VMEM)
    hbm = pl.BlockSpec(memory_space=pl.ANY)
    dma = pltpu.SemaphoreType.DMA
    near, far = PLANE - 1, NZ - 1
    return pl.pallas_call(
        kernel,
        out_shape=(
            jax.ShapeDtypeStruct((NC, PLANE, K, K), BF16),
            jax.ShapeDtypeStruct((ROWS, K), F32),
        ),
        in_specs=[hbm, hbm],
        out_specs=(hbm, vmem),
        scratch_shapes=[
            pltpu.VMEM((NC, ROWS, HALF), BF16),
            pltpu.VMEM((ROWS, HALF), BF16),
            pltpu.VMEM((D, K), BF16),
            pltpu.VMEM((NC, K, ROWS), F32),
            pltpu.VMEM((NX, NY, K, K), F32),
            pltpu.VMEM((PLANE, K, K), BF16),
            pltpu.VMEM((NX - 1, NY, K // 2, K), F32),
            pltpu.VMEM((NY - 1, NX, K // 2, K), F32),
            pltpu.VMEM((NY, K // 2, K), F32),
            pltpu.VMEM((NX, K // 2, K), F32),
            pltpu.VMEM((NY - 1, K // 2, K), F32),
            pltpu.VMEM((NX - 1, K // 2, K), F32),
            pltpu.VMEM((ITERS, near, K, K), BF16),
            pltpu.VMEM((NZ, PIECE, K), F32),
            pltpu.VMEM((STEPS, far, PIECE, K), F32),
            pltpu.VMEM((STEPS, NZ, PIECE, K), F32),
            pltpu.VMEM((NX, NY, K, K), F32),
            pltpu.VMEM((ITERS, PLANE, K, K), BF16),
            pltpu.VMEM((PLANE, 8, K), F32),
            pltpu.VMEM((STEPS, near, 8, K), F32),
            pltpu.VMEM((STEPS, NZ, 8, K), F32),
            pltpu.VMEM((STEPS, PLANE, 8, K), F32),
            pltpu.VMEM((K, K), F32),
            pltpu.VMEM((K, K), F32),
            pltpu.VMEM((K, K), F32),
            pltpu.VMEM((ITERS, K, K), F32),
            pltpu.VMEM((NC, K, ROWS), F32),
            pltpu.VMEM((ITERS, NC, K, ROWS), F32),
            dma((3,)), dma((4,)), dma((8, 2)),
            dma((STEPS, 2)), dma((STEPS, 2)), dma((STEPS, 2)), dma((STEPS, 2)),
            dma((STEPS, 2)), dma((STEPS, 2)), dma((STEPS, 2)),
            dma((ITERS, 2)), dma((ITERS, 2)),
            dma((2, near)), dma((PLANE,)), dma((PLANE,)), dma((PLANE,)),
        ],
        compiler_params=pltpu.CompilerParams(
            collective_id=0, has_side_effects=True, vmem_limit_bytes=62 * 2**20
        ),
        name="sweep",
    )(embeddings, sketch)


def finish_kernel(proj_ref, basis_ref, basis_out, proj_out):
    proj_out[...] = proj_ref[...].astype(F32)
    basis_out[...] = basis_ref[...]


def finish(projected, basis):
    steps = 2
    tall = pl.BlockSpec((D // steps, K), lambda i: (i, 0))
    short = pl.BlockSpec((ROWS // steps, K), lambda i: (i, 0))
    return pl.pallas_call(
        finish_kernel,
        grid=(steps,),
        out_shape=(
            jax.ShapeDtypeStruct((ROWS, K), F32),
            jax.ShapeDtypeStruct((D, K), F32),
        ),
        in_specs=[tall, short],
        out_specs=(short, tall),
        name="finish",
    )(projected, basis)


def per_device(embeddings, sketch):
    projected, basis = sweep(embeddings, sketch)
    return finish(projected.reshape(D, K), basis)


def solution(mesh):
    return jax.shard_map(
        per_device,
        mesh=mesh,
        in_specs=(P(("grp", "row"), None), P()),
        out_specs=(P(("grp", "row"), None), P()),
        check_vma=False,
    )
```
